512 devices in a mesh: mem: 16 (over z), slab: 32 (over y, x, core).
Axes of the slice: x: 4, y: 4, z: 16, core: 2. Of those that a mesh axis runs over, the one named last changes fastest.
Arguments:
- ensemble: float32 [256, 4096, 128], P('mem', 'slab'), may hold values from -6 to 6
- diffusivity: float32 [4096, 128], P('slab'), may hold values from 0.15 to 0.25
- velocity: float32 [2, 4096, 128], P(None, 'slab'), may hold values from -0.5 to 0.5
- obs_value: float32 [655360], P(('mem', 'slab')), may hold values from -6 to 6
- obs_weight: float32 [655360], P(('mem', 'slab')), may hold values from 0.3 to 12
- obs_slab: int32 [655360, 1], P(('mem', 'slab')), may hold values from 0 to 31; in each aligned block of 1280 rows (0 to 1279, 1280 to 2559, ...) at most 80 rows name the same one
- obs_cell: int32 [655360], P(('mem', 'slab')), may hold values from 0 to 1023
Outputs:
- analysis: float32 [256, 4096, 128], P('mem', 'slab')
The draws below stay inside these ranges and needn't reach their ends.
Inputs may be any that keep to these rules, and one draw needn't show every extreme that they name: `obs_slab`: among the 1280 observations stored on one device, no slab is named more than 80 times; on some device one slab is named exactly 80 times.
All inputs are finite; a program needn't handle non-finite values.
Results may differ from the reference program's by a relative error of at most 0.0085.
Values sent between devices are 32-bit elements; how exact they have to be, the bound alone decides.
A program may use at most 128 MiB of HBM per device.

```python
import math
import jax
import jax.numpy as jnp
import numpy as np
from jax import lax

M = 256
GX = 128
PATCH_DEV = 8
STEPS = 4
NS_STEPS = 5
OBS_DEV = 1280
CAP = 80
ROWS_DEV = 128
GY = 4096
NOBS = 655360
N_MEM = 16
N_SLAB = 32


def with_ends(array, own_key, smallest, largest):
    index_at = [jax.random.randint(jax.random.fold_in(own_key, axis), (), 0, length) for axis, length in enumerate(array.shape)]
    longest = array.shape.index(max(array.shape))
    neighbour = index_at[:longest] + [(index_at[longest] + 1) % array.shape[longest]] + index_at[longest + 1:]
    return array.at[tuple(index_at)].set(smallest).at[tuple(neighbour)].set(largest)


def levels(stream_key, shape, split, smallest, high):
    gain = 1.0
    for axis_at, parts in split:
        steps = jax.random.uniform(jax.random.fold_in(jax.random.fold_in(stream_key, 6), axis_at), (parts,), jnp.float32, smallest / len(split), high / len(split))
        gain = gain * jnp.repeat(jnp.exp(steps), shape[axis_at] // parts).reshape((-1,) + (1,) * (len(shape) - 1 - axis_at))
    return gain


def routed_block(own_key, own, number, rows, count, top, bound, lean):
    sequence = jax.random.permutation(own_key, count)
    packed, ordinary = portions_of(count, rows * top, bound, lean, True), portions_of(count, rows * top, bound, lean, False)
    places = jnp.arange(count)

    def named(tallies, turn):
        used = int((tallies > 0).sum())
        fixed = max(1, used // 4)
        passed = fixed + (places - fixed + turn * (used - fixed)) % max(1, count - fixed)
        return jnp.zeros((count,), jnp.int32).at[sequence[jnp.where(places < fixed, places, passed)]].set(jnp.asarray(tallies, jnp.int32))

    tallies = jnp.where(number % 4 == 0, named(packed, number // 4), named(ordinary, number - number // 4 - 1))
    mixed = jax.random.permutation(jax.random.fold_in(own, 3), count)
    donor, taker = mixed[0:count // 2 * 2:2], mixed[1:count // 2 * 2:2]
    slack = jnp.minimum(tallies[donor] - 1, bound - tallies[taker]) // 2
    slack = jnp.where((donor == sequence[0]) | (taker == sequence[0]) | (tallies[taker] == 0), 0, jnp.maximum(slack, 0))
    passed = jax.random.randint(jax.random.fold_in(own, 4), (count // 2,), 0, 1 << 20) % (slack + 1)
    tallies = tallies.at[donor].add(-passed).at[taker].add(passed)
    labels = jnp.searchsorted(jnp.cumsum(tallies), jnp.arange(rows * top), side="right").astype(jnp.int32)
    table = labels.reshape(top, rows).T
    table = table[jax.random.permutation(jax.random.fold_in(own, 1), rows)]
    turn = jax.random.randint(jax.random.fold_in(own, 2), (rows, 1), 0, top)
    return jnp.take_along_axis(table, (jnp.arange(top)[None, :] + turn) % top, axis=1)


def portions_of(count, total, reach, lean, full):
    weights = [(1 << 20) // math.isqrt(standing ** lean) + 1 for standing in range(1, count + 1)]
    largest = reach if full else min(reach, max(-(-total // count), total * weights[0] // sum(weights)))
    least = 1 if total - largest >= count - 1 else 0
    given, spare = [largest] + [least] * (count - 1), total - largest - least * (count - 1)
    while spare > 0:
        free = [i for i in range(1, count) if given[i] < largest] or [i for i in range(1, count) if given[i] < reach]
        pool, budget = sum([weights[i] for i in free]), spare
        for i in free:
            extra = min(reach - given[i], max(1, budget * weights[i] // pool), spare)
            given[i] = given[i] + extra
            spare = spare - extra
    return np.array(given)


def gaussian(key, extent, deviation, limit, split=(), held_as=jnp.bfloat16):
    array = deviation * jax.random.normal(key, extent, jnp.float32)
    if split:
        array = array * levels(key, extent, split, -0.22, 0.18)
    return jnp.clip(array, -limit, limit).astype(held_as)


def setup_inputs(seed: int = 0) -> dict:
    splits = jax.random.split(jax.random.key(seed), 8)
    ensemble = gaussian(splits[0], (M, GY, GX), 1.0, 6.0, ((0, 16), (1, 32)), jnp.float32)
    diffusivity = jnp.clip(0.15 + 0.099999994 * jax.random.uniform(splits[1], (GY, GX), jnp.float32) ** levels(splits[1], (GY, GX), ((0, 32),), -0.2, 0.2), 0.15, 0.25)
    velocity = jnp.clip(jax.random.uniform(splits[2], (2, GY, GX), jnp.float32, -0.5, 0.5) * levels(splits[2], (2, GY, GX), ((1, 32),), -0.4, 0.0), -0.5, 0.5)
    obs_value = gaussian(splits[3], (NOBS,), 1.0, 6.0, ((0, 512),), jnp.float32)
    obs_weight = jnp.clip(jnp.exp(math.log(12.0) - 3.6888794 * jax.random.uniform(splits[4], (NOBS,), jnp.float32) ** levels(splits[4], (NOBS,), ((0, 512),), -0.2, 0.2)), 0.3, 12.0)
    obs_slab_keys = jax.random.split(jax.random.fold_in(splits[5], 1), NOBS // OBS_DEV)
    obs_slab_turns = jax.random.permutation(jax.random.fold_in(splits[5], 3), NOBS // OBS_DEV)
    obs_slab = jax.vmap(lambda own, number: routed_block(jax.random.fold_in(splits[5], 2), own, number, OBS_DEV, N_SLAB, 1, CAP, 2))(obs_slab_keys, obs_slab_turns).reshape((NOBS, 1))
    obs_cell = with_ends(jax.random.randint(splits[6], (NOBS,), 0, PATCH_DEV * GX), jax.random.fold_in(splits[6], 1), 0, (PATCH_DEV * GX) - 1).astype(jnp.int32)
    return dict(ensemble=ensemble, diffusivity=diffusivity, velocity=velocity, obs_value=obs_value, obs_weight=obs_weight, obs_slab=obs_slab, obs_cell=obs_cell)


def stencil(center, upper_row, lower_row, diffuse, drift_x, drift_y):
    east_side = jnp.roll(center, -1, axis=-1)
    west_side = jnp.roll(center, 1, axis=-1)
    laplace = east_side + west_side + upper_row + lower_row - 4.0 * center
    return center + diffuse * laplace - 0.5 * drift_x * (east_side - west_side) - 0.5 * drift_y * (lower_row - upper_row)

def analyse(fields, obs_vals, obs_wts, obs_cells):
    members, patches, width = fields.shape
    center_mean = lax.optimization_barrier(jnp.mean(fields, axis=0))
    spread = (fields - center_mean[None]).astype(jnp.bfloat16)
    flat_mean = center_mean.reshape(-1)
    at_obs = jnp.take(spread.reshape(members, -1), obs_cells, axis=1)
    misfit = obs_vals - jnp.take(flat_mean, obs_cells)
    patch_of = obs_cells // width
    weights = obs_wts[None, :] * (patch_of[None, :] == jnp.arange(patches, dtype=jnp.int32)[:, None]).astype(jnp.float32)
    weighted = (at_obs[None].astype(jnp.float32) * weights[:, None, :]).astype(jnp.bfloat16)
    gram = jnp.einsum('pmo,no->pmn', weighted.astype(jnp.float32), at_obs.astype(jnp.float32), precision=lax.Precision.HIGHEST)
    eye_f = jnp.eye(members, dtype=jnp.float32)
    system = (members - 1) * eye_f[None] + gram
    scale = 8.0 * jnp.sqrt(lax.optimization_barrier(jnp.sum(system * system, axis=(1, 2))) / members)
    iterate = (system / scale[:, None, None]).astype(jnp.bfloat16)
    inverse_root = jnp.broadcast_to(eye_f.astype(jnp.bfloat16), iterate.shape)
    for sweep in range(NS_STEPS):
        product = jnp.einsum('pij,pjk->pik', inverse_root.astype(jnp.float32), iterate.astype(jnp.float32), precision=lax.Precision.HIGHEST)
        factor = (1.5 * eye_f[None] - 0.5 * product).astype(jnp.bfloat16)
        iterate = jnp.einsum('pij,pjk->pik', iterate.astype(jnp.float32), factor.astype(jnp.float32), precision=lax.Precision.HIGHEST).astype(jnp.bfloat16)
        inverse_root = jnp.einsum('pij,pjk->pik', factor.astype(jnp.float32), inverse_root.astype(jnp.float32), precision=lax.Precision.HIGHEST).astype(jnp.bfloat16)
    root_f = inverse_root.astype(jnp.float32)
    pull = jnp.dot(at_obs.astype(jnp.float32), (weights * misfit[None, :]).T, precision=lax.Precision.HIGHEST)
    first = jnp.einsum('pij,jp->pi', root_f, pull, precision=lax.Precision.HIGHEST)
    mean_gain = jnp.einsum('pij,pj->pi', root_f, first, precision=lax.Precision.HIGHEST) / scale[:, None]
    transform = (jnp.sqrt((members - 1) / scale)[:, None, None] * root_f + mean_gain[:, None, :]).astype(jnp.bfloat16)
    update = jnp.einsum('pik,kpx->ipx', transform.astype(jnp.float32), spread.astype(jnp.float32), precision=lax.Precision.HIGHEST)
    return center_mean[None] + update

def reference(ensemble, diffusivity, velocity, obs_value, obs_weight, obs_slab, obs_cell):
    fields = ensemble
    for step in range(STEPS):
        fields = stencil(fields, jnp.roll(fields, 1, axis=1), jnp.roll(fields, -1, axis=1), diffusivity, velocity[0], velocity[1])
    row_vals = obs_value.reshape(N_MEM, N_SLAB * OBS_DEV)
    row_wts = obs_weight.reshape(N_MEM, N_SLAB * OBS_DEV)
    row_slab = obs_slab[:, 0].reshape(N_MEM, N_SLAB * OBS_DEV)
    row_cell = obs_cell.reshape(N_MEM, N_SLAB * OBS_DEV)

    def one_device(index):
        mem_id = index // N_SLAB
        slab_id = index % N_SLAB
        start = (slab_id * ROWS_DEV + mem_id * PATCH_DEV).astype(jnp.int32)
        block = lax.dynamic_slice_in_dim(fields, start, PATCH_DEV, 1)
        wanted = row_slab[mem_id] == slab_id
        ranking = jnp.argsort(1 - wanted.astype(jnp.int32), stable=True)[:N_SLAB * CAP]
        keep = wanted[ranking]
        obs_vals = jnp.where(keep, row_vals[mem_id][ranking], 0.0)
        obs_wts = jnp.where(keep, row_wts[mem_id][ranking], 0.0)
        obs_cells = jnp.where(keep, row_cell[mem_id][ranking], 0).astype(jnp.int32)
        return analyse(block, obs_vals, obs_wts, obs_cells)
    stacked = lax.map(one_device, jnp.arange(N_MEM * N_SLAB, dtype=jnp.int32))
    return stacked.reshape(N_MEM, N_SLAB, M, PATCH_DEV, GX).transpose(2, 1, 0, 3, 4).reshape(M, GY, GX)
```

```python
import jax
import jax.numpy as jnp
from jax import lax
from jax.experimental import pallas as pl
from jax.experimental.pallas import tpu as pltpu
from jax.sharding import PartitionSpec as P

STEPS = 4
NS_STEPS = 5
NM = 16
NS = 32
K = 8
M = 256
ML = 16
W = 128
OBS = 1280
MESH = pl.DeviceIdType.MESH
F32 = jnp.float32
BF16 = jnp.bfloat16
ORDER = (8, 7, 9, 6, 10, 5, 11, 4, 12, 3, 13, 2, 14, 1, 15)


def dot(a, b, dims):
    return lax.dot_general(a, b, (dims, ((), ())), preferred_element_type=F32)


def nn(a, b):
    return dot(a, b, ((1,), (0,)))


def nt(a, b):
    return dot(a, b, ((1,), (1,)))


def parts(x):
    hi = x.astype(BF16).astype(F32)
    rest = x - hi
    mid = rest.astype(BF16).astype(F32)
    return hi, mid, rest - mid


def row_times(row, mat_t):
    hi, mid, lo = parts(row)
    n = row.shape[1]
    at = lax.broadcasted_iota(jnp.int32, (16, n), 0)
    stack = jnp.where(at == 0, hi, jnp.where(at == 1, mid, jnp.where(at == 2, lo, 0.0)))
    return jnp.sum(nt(stack.astype(BF16), mat_t), axis=0, keepdims=True)


def advance(x, coeffs):
    rows = x.shape[0]
    for _ in range(STEPS):
        x = (
            coeffs[0] * x
            + coeffs[1] * pltpu.roll(x, W - 1, 1)
            + coeffs[2] * pltpu.roll(x, 1, 1)
            + coeffs[3] * pltpu.roll(x, 1, 0)
            + coeffs[4] * pltpu.roll(x, rows - 1, 0)
        )
    return x


def combine(d, vx, vy):
    ax, ay = 0.5 * vx, 0.5 * vy
    return 1.0 - 4.0 * d, d - ax, d + ax, d + ay, d - ay


def kernel(
    ens_ref, dif_ref, vel_ref, val_ref, wt_ref, slab_ref, cell_ref, out_ref,
    ens, cf, cfe, hs, hr, send, recv, ana, ret, tab, orx, wtot, utot,
    ens_sem, hs_sem, hr_sem, fs_sem, fr_sem, rs_sem, rr_sem, os_sem, or_sem,
):
    me = lax.axis_index("mem")
    sl = lax.axis_index("slab")

    def mem_peer(d):
        return lax.rem(me + d, NM)

    load = pltpu.make_async_copy(ens_ref, ens, ens_sem)
    load.start()
    bar = pltpu.get_barrier_semaphore()

    @pl.loop(1, NM)
    def _(d):
        pl.semaphore_signal(bar, inc=1, device_id={"mem": mem_peer(d)}, device_id_type=MESH)

    @pl.loop(1, NS)
    def _(d):
        pl.semaphore_signal(
            bar, inc=1, device_id={"slab": lax.rem(sl + d, NS)}, device_id_type=MESH
        )

    dif, vx, vy = dif_ref[...], vel_ref[0], vel_ref[1]
    for i, c in enumerate(combine(dif, vx, vy)):
        cf[i] = c
    hs[0, 16], hs[1, 16] = dif[0:8], dif[120:128]
    hs[0, 17], hs[1, 17] = vx[0:8], vx[120:128]
    hs[0, 18], hs[1, 18] = vy[0:8], vy[120:128]
    load.wait()

    @pl.loop(0, ML)
    def _(m):
        x = ens[m]
        hs[0, m] = x[0:8]
        hs[1, m] = x[120:128]

    @pl.loop(0, ML)
    def _(m):
        x = advance(ens[m], cf)
        for q in range(1, NM - 1):
            send[q, pl.ds(m, K, stride=ML), :] = x[q * 8 : q * 8 + 8]

    pl.semaphore_wait(bar, NM - 1 + NS - 1)

    up = lax.rem(sl + NS - 1, NS)
    down = lax.rem(sl + 1, NS)

    def halo(side, to):
        return pltpu.make_async_remote_copy(
            src_ref=hs.at[side], dst_ref=hr.at[1 - side],
            send_sem=hs_sem.at[side], recv_sem=hr_sem.at[1 - side],
            device_id={"slab": to}, device_id_type=MESH,
        )

    halo(0, up).start()
    halo(1, down).start()

    def forward(k, d):
        q = mem_peer(d)
        return pltpu.make_async_remote_copy(
            src_ref=send.at[q, pl.ds(pl.multiple_of(k * ML, ML), ML)],
            dst_ref=recv.at[k, pl.ds(pl.multiple_of(me * ML, ML), ML)],
            send_sem=fs_sem.at[k, d], recv_sem=fr_sem.at[k, me],
            device_id={"mem": q}, device_id_type=MESH,
        )

    def forward_from(k, d):
        q = mem_peer(d)
        return pltpu.make_async_remote_copy(
            src_ref=send.at[q, pl.ds(pl.multiple_of(k * ML, ML), ML)],
            dst_ref=recv.at[k, pl.ds(pl.multiple_of(q * ML, ML), ML)],
            send_sem=fs_sem.at[k, d], recv_sem=fr_sem.at[k, q],
            device_id={"mem": q}, device_id_type=MESH,
        )

    def at_edge(q):
        return jnp.logical_or(q == 0, q == NM - 1)

    @pl.loop(0, K)
    def _(k):
        for d in ORDER:

            @pl.when(jnp.logical_not(at_edge(mem_peer(d))))
            def _():
                forward(k, d).start()

    wt, val = wt_ref[...], val_ref[...]
    mine = lax.broadcasted_iota(jnp.int32, (NS, OBS), 0) == slab_ref[...]
    rows = [jnp.where(mine, piece, 0.0) for piece in parts(wt) + parts(wt * val)]
    left = jnp.concatenate(rows, axis=0).astype(BF16)
    cell = cell_ref[...]
    column = lax.broadcasted_iota(jnp.int32, (W, OBS), 0)
    for p in range(K):
        hot = jnp.where(column + p * W == cell, 1.0, 0.0).astype(BF16)
        sums = nt(left, hot)
        tab[:, p, :] = sums[0:NS] + sums[NS : 2 * NS] + sums[2 * NS : 3 * NS]
        tab[:, K + p, :] = sums[3 * NS : 4 * NS] + sums[4 * NS : 5 * NS] + sums[5 * NS : 6 * NS]

    def route(d):
        to = lax.rem(sl + d, NS)
        return pltpu.make_async_remote_copy(
            src_ref=tab.at[to], dst_ref=orx.at[sl], send_sem=os_sem.at[d], recv_sem=or_sem.at[sl],
            device_id={"slab": to}, device_id_type=MESH,
        )

    def route_from(d):
        to = lax.rem(sl + d, NS)
        return pltpu.make_async_remote_copy(
            src_ref=tab.at[to], dst_ref=orx.at[to], send_sem=os_sem.at[d], recv_sem=or_sem.at[to],
            device_id={"slab": to}, device_id_type=MESH,
        )

    @pl.loop(1, NS)
    def _(d):
        route(d).start()

    orx[sl] = tab[sl]

    pltpu.make_async_remote_copy(
        src_ref=hs.at[0], dst_ref=hr.at[0], send_sem=hs_sem.at[0], recv_sem=hr_sem.at[0],
        device_id={"slab": up}, device_id_type=MESH,
    ).wait_recv()
    pltpu.make_async_remote_copy(
        src_ref=hs.at[1], dst_ref=hr.at[1], send_sem=hs_sem.at[1], recv_sem=hr_sem.at[1],
        device_id={"slab": down}, device_id_type=MESH,
    ).wait_recv()

    def edge(top, a, b, bottom):
        return jnp.concatenate([top, a, b, bottom], axis=0)

    edge_d = edge(hr[0, 16], dif[0:16], dif[112:128], hr[1, 16])
    edge_x = edge(hr[0, 17], vx[0:16], vx[112:128], hr[1, 17])
    edge_y = edge(hr[0, 18], vy[0:16], vy[112:128], hr[1, 18])
    for i, c in enumerate(combine(edge_d, edge_x, edge_y)):
        cfe[i] = c

    @pl.loop(0, ML)
    def _(m):
        x = edge(hr[0, m], ens[m, 0:16, :], ens[m, 112:128, :], hr[1, m])
        x = advance(x, cfe)
        send[0, pl.ds(m, K, stride=ML), :] = x[8:16]
        send[NM - 1, pl.ds(m, K, stride=ML), :] = x[32:40]

    @pl.loop(0, K)
    def _(k):
        for d in ORDER:

            @pl.when(at_edge(mem_peer(d)))
            def _():
                forward(k, d).start()

    @pl.loop(0, K)
    def _(k):
        recv[k, pl.ds(pl.multiple_of(me * ML, ML), ML), :] = send[
            me, pl.ds(pl.multiple_of(k * ML, ML), ML), :
        ]

    @pl.loop(1, NS)
    def _(d):
        route_from(d).wait_recv()

    totals = orx[0]
    for s in range(1, NS):
        totals = totals + orx[s]
    wtot[...] = totals[0:K]
    utot[...] = totals[K : 2 * K]

    def back(k, d):
        q = mem_peer(d)
        return pltpu.make_async_remote_copy(
            src_ref=ana.at[k, pl.ds(pl.multiple_of(q * ML, ML), ML)],
            dst_ref=ret.at[me, pl.ds(pl.multiple_of(k * ML, ML), ML)],
            send_sem=rs_sem.at[k, d], recv_sem=rr_sem.at[k, me],
            device_id={"mem": q}, device_id_type=MESH,
        )

    def back_from(k, d):
        q = mem_peer(d)
        return pltpu.make_async_remote_copy(
            src_ref=ana.at[k, pl.ds(pl.multiple_of(q * ML, ML), ML)],
            dst_ref=ret.at[q, pl.ds(pl.multiple_of(k * ML, ML), ML)],
            send_sem=rs_sem.at[k, d], recv_sem=rr_sem.at[k, q],
            device_id={"mem": q}, device_id_type=MESH,
        )

    eye = jnp.where(
        lax.broadcasted_iota(jnp.int32, (M, M), 0) == lax.broadcasted_iota(jnp.int32, (M, M), 1),
        1.0, 0.0,
    )

    @pl.loop(0, K)
    def _(k):
        @pl.loop(1, NM)
        def _(d):
            forward_from(k, d).wait_recv()

        x = recv[k]
        mean = jnp.sum(x, axis=0, keepdims=True) * (1.0 / M)
        spread = (x - mean).astype(BF16)
        weight = wtot[pl.ds(k, 1), :]
        weighted = (spread.astype(F32) * weight).astype(BF16)
        system = (M - 1.0) * eye + nt(weighted, spread)
        squares = jnp.sum(jnp.sum(system * system, axis=0, keepdims=True), axis=1, keepdims=True)
        scale = 8.0 * jnp.sqrt(squares * (1.0 / M))
        pull = row_times(utot[pl.ds(k, 1), :] - weight * mean, spread)
        iterate = (system * (1.0 / scale)).astype(BF16)
        root = (1.5 * eye - 0.5 * iterate.astype(F32)).astype(BF16)
        iterate = nn(iterate, root).astype(BF16)
        for sweep in range(1, NS_STEPS):
            factor = (1.5 * eye - 0.5 * nn(root, iterate)).astype(BF16)
            if sweep < NS_STEPS - 1:
                iterate = nn(iterate, factor).astype(BF16)
            root = nn(factor, root).astype(BF16)
        gain = row_times(row_times(pull, root), root) * (1.0 / scale)
        transform = (jnp.sqrt((M - 1.0) / scale) * root.astype(F32) + gain).astype(BF16)
        ana[k] = mean + nn(transform, spread)
        for d in ORDER:
            back(k, d).start()
        ret[me, pl.ds(pl.multiple_of(k * ML, ML), ML), :] = ana[
            k, pl.ds(pl.multiple_of(me * ML, ML), ML), :
        ]

    @pl.loop(0, K)
    def _(k):
        @pl.loop(1, NM)
        def _(d):
            back_from(k, d).wait_recv()

    @pl.loop(0, ML)
    def _(m):
        for q in range(NM):
            out_ref[m, q * 8 : q * 8 + 8, :] = ret[q, pl.ds(m, K, stride=ML), :]

    halo(0, up).wait_send()
    halo(1, down).wait_send()

    @pl.loop(1, NS)
    def _(d):
        route(d).wait_send()

    @pl.loop(0, K)
    def _(k):
        @pl.loop(1, NM)
        def _(d):
            forward(k, d).wait_send()
            back(k, d).wait_send()


def shards(ensemble, diffusivity, velocity, obs_value, obs_weight, obs_slab, obs_cell):
    vmem = pl.BlockSpec(memory_space=pltpu.VMEM)
    dma = pltpu.SemaphoreType.DMA
    return pl.pallas_call(
        kernel,
        out_shape=jax.ShapeDtypeStruct((ML, NM * K, W), F32),
        in_specs=[pl.BlockSpec(memory_space=pl.ANY)] + [vmem] * 6,
        out_specs=vmem,
        scratch_shapes=[
            pltpu.VMEM((ML, NM * K, W), F32),
            pltpu.VMEM((5, NM * K, W), F32),
            pltpu.VMEM((5, 48, W), F32),
            pltpu.VMEM((2, ML + 3, 8, W), F32),
            pltpu.VMEM((2, ML + 3, 8, W), F32),
            pltpu.VMEM((NM, K * ML, W), F32),
            pltpu.VMEM((K, M, W), F32),
            pltpu.VMEM((K, M, W), F32),
            pltpu.VMEM((NM, K * ML, W), F32),
            pltpu.VMEM((NS, 2 * K, W), F32),
            pltpu.VMEM((NS, 2 * K, W), F32),
            pltpu.VMEM((K, W), F32),
            pltpu.VMEM((K, W), F32),
            dma,
            dma((2,)),
            dma((2,)),
            dma((K, NM)),
            dma((K, NM)),
            dma((K, NM)),
            dma((K, NM)),
            dma((NS,)),
            dma((NS,)),
        ],
        compiler_params=pltpu.CompilerParams(
            collective_id=0, has_side_effects=True, vmem_limit_bytes=40 * 2**20
        ),
    )(
        ensemble,
        diffusivity,
        velocity,
        obs_value.reshape(1, OBS),
        obs_weight.reshape(1, OBS),
        obs_slab.reshape(1, OBS),
        obs_cell.reshape(1, OBS),
    )


def solution(mesh):
    return jax.shard_map(
        shards,
        mesh=mesh,
        in_specs=(
            P("mem", "slab", None),
            P("slab", None),
            P(None, "slab", None),
            P(("mem", "slab")),
            P(("mem", "slab")),
            P(("mem", "slab"), None),
            P(("mem", "slab")),
        ),
        out_specs=P("mem", "slab", None),
        check_vma=False,
    )
```

```python
import jax
import jax.numpy as jnp
from jax import lax
from jax.experimental import pallas as pl
from jax.experimental.pallas import tpu as pltpu
from jax.sharding import PartitionSpec as P

STEPS = 4
NS_STEPS = 5
NM = 16
NS = 32
K = 8
M = 256
ML = 16
W = 128
OBS = 1280
ROWS = 128
HALO = 4
EARLY = 2
PIECES, STRIDE, QS = 3, 40, 5
MESH = pl.DeviceIdType.MESH
F32 = jnp.float32
BF16 = jnp.bfloat16
ORDER = (8, 7, 9, 6, 10, 5, 11, 4, 12, 3, 13, 2, 14, 1, 15)


def dot(a, b, dims):
    return lax.dot_general(a, b, (dims, ((), ())), preferred_element_type=F32)


def nn(a, b):
    return dot(a, b, ((1,), (0,)))


def nt(a, b):
    return dot(a, b, ((1,), (1,)))


def parts(x):
    hi = x.astype(BF16).astype(F32)
    rest = x - hi
    mid = rest.astype(BF16).astype(F32)
    return hi, mid, rest - mid


def row_times(row, mat_t):
    hi, mid, lo = parts(row)
    n = row.shape[1]
    at = lax.broadcasted_iota(jnp.int32, (16, n), 0)
    stack = jnp.where(at == 0, hi, jnp.where(at == 1, mid, jnp.where(at == 2, lo, 0.0)))
    return jnp.sum(nt(stack.astype(BF16), mat_t), axis=0, keepdims=True)


def advance(src, dst, cx, at, rows, shift=0):
    for r in range(rows):
        c = [cx[i, at + r] for i in range(5)]
        for h in range(2):
            x = src[at + r, h]
            dst[at + r + shift, h] = (
                (c[0] * x + c[3] * src[at + r - 1, h])
                + (c[4] * src[at + r + 1, h] + c[1] * pltpu.roll(x, W - 1, 1))
                + c[2] * pltpu.roll(x, 1, 1)
            )


def combine(d, vx, vy):
    ax, ay = 0.5 * vx, 0.5 * vy
    return 1.0 - 4.0 * d, d - ax, d + ax, d + ay, d - ay


def kernel(
    ens_hbm, dif_hbm, vel_hbm, val_hbm, wt_hbm, slab_hbm, cell_hbm, out_ref,
    ens, dif_ref, vel_ref, val_ref, wt_ref, slab_ref, cell_ref, b0, b1, b2, b3, cx, cs, cr, send, recv, ana, ret, tab, orx, wtot, utot,
    in_sem, hs_sem, hr_sem, cs_sem, cr_sem, fs_sem, fr_sem, rs_sem, rr_sem, os_sem, or_sem,
):
    me = lax.axis_index("mem")
    sl = lax.axis_index("slab")

    def mem_peer(d):
        return lax.rem(me + d, NM)

    pairs = (
        (dif_hbm, dif_ref), (vel_hbm, vel_ref), (ens_hbm, ens),
        (wt_hbm, wt_ref), (val_hbm, val_ref), (slab_hbm, slab_ref), (cell_hbm, cell_ref),
    )
    loads = [pltpu.make_async_copy(a, b, in_sem.at[i]) for i, (a, b) in enumerate(pairs)]
    for load in loads:
        load.start()
    bar = pltpu.get_barrier_semaphore()

    @pl.loop(1, NM)
    def _(d):
        pl.semaphore_signal(bar, inc=1, device_id={"mem": mem_peer(d)}, device_id_type=MESH)

    @pl.loop(1, NS)
    def _(d):
        pl.semaphore_signal(
            bar, inc=1, device_id={"slab": lax.rem(sl + d, NS)}, device_id_type=MESH
        )

    loads[0].wait()
    loads[1].wait()
    for i, ref in enumerate((dif_ref, vel_ref.at[0], vel_ref.at[1])):
        cs[0, i] = ref[0:8]
        cs[1, i] = ref[120:128]

    def expand(at, rows, d, vx, vy):
        for i, c in enumerate(combine(d, vx, vy)):
            cx[i, pl.ds(at, rows)] = jnp.broadcast_to(c[:, None, :], (rows, 8, W))

    @pl.loop(0, NM)
    def _(b):
        own = pl.ds(pl.multiple_of(b * 8, 8), 8)
        expand(HALO + b * 8, 8, dif_ref[own], vel_ref[0, own], vel_ref[1, own])

    loads[2].wait()

    @pl.loop(0, NM)
    def _(b):
        for h in range(2):
            tiles = [
                ens[pl.ds(pl.multiple_of((h * 8 + m) * ROWS + b * 8, 8), 8), :] for m in range(8)
            ]
            b0[pl.ds(HALO + b * 8, 8), h] = jnp.swapaxes(jnp.stack(tiles, axis=0), 0, 1)

    up = lax.rem(sl + NS - 1, NS)
    down = lax.rem(sl + 1, NS)

    def halo(side, to):
        start, land = ((HALO, HALO + ROWS), (ROWS, 0))[side]
        fields = pltpu.make_async_remote_copy(
            src_ref=b0.at[pl.ds(start, HALO)], dst_ref=b0.at[pl.ds(land, HALO)],
            send_sem=hs_sem.at[side], recv_sem=hr_sem.at[side],
            device_id={"slab": to}, device_id_type=MESH,
        )
        coeffs = pltpu.make_async_remote_copy(
            src_ref=cs.at[side], dst_ref=cr.at[side],
            send_sem=cs_sem.at[side], recv_sem=cr_sem.at[side],
            device_id={"slab": to}, device_id_type=MESH,
        )
        return fields, coeffs

    halos = halo(0, up) + halo(1, down)

    def forward(k, d):
        q = mem_peer(d)
        return pltpu.make_async_remote_copy(
            src_ref=send.at[q * K + k], dst_ref=recv.at[k, pl.ds(2 * me, 2)],
            send_sem=fs_sem.at[k, d], recv_sem=fr_sem.at[k, me],
            device_id={"mem": q}, device_id_type=MESH,
        )

    def forward_from(k, d):
        q = mem_peer(d)
        return pltpu.make_async_remote_copy(
            src_ref=send.at[q * K + k], dst_ref=recv.at[k, pl.ds(2 * q, 2)],
            send_sem=fs_sem.at[k, d], recv_sem=fr_sem.at[k, q],
            device_id={"mem": q}, device_id_type=MESH,
        )

    def at_edge(k, q):
        return q == 0 if k < HALO else q == NM - 1

    states = (b0, b1, b2, b3, send)

    @pl.loop(0, PIECES)
    def _(b):
        for step in range(STEPS):
            first = HALO + step + 1
            rows = ROWS - 2 * step - 2 - (PIECES - 1) * STRIDE
            shift = -HALO if step == STEPS - 1 else 0
            advance(states[step], states[step + 1], cx, first + b * STRIDE, rows, shift)

        @pl.when(b == 0)
        def _():
            pl.semaphore_wait(bar, NM - 1 + NS - 1)
            for copy in halos:
                copy.start()

        for k in range(EARLY):
            for i in range(QS):
                q = b * QS + i

                @pl.when(jnp.logical_and(q != me, jnp.logical_not(at_edge(k, q))))
                def _():
                    forward(k, lax.rem(q - me + NM, NM)).start()

    for load in loads[3:]:
        load.wait()

    def row(ref):
        return jnp.concatenate([ref[i : i + 1, :] for i in range(OBS // W)], axis=1)

    wt, val, cell = row(wt_ref), row(val_ref), row(cell_ref)
    mine = lax.broadcasted_iota(jnp.int32, (NS, OBS), 0) == slab_ref[...]
    rows = [jnp.where(mine, piece, 0.0) for piece in parts(wt) + parts(wt * val)]
    left = jnp.concatenate(rows, axis=0).astype(BF16)
    column = lax.broadcasted_iota(jnp.int32, (W, OBS), 0)
    for p in range(K):
        hot = jnp.where(column + p * W == cell, 1.0, 0.0).astype(BF16)
        sums = nt(left, hot)
        tab[:, p, :] = sums[0:NS] + sums[NS : 2 * NS] + sums[2 * NS : 3 * NS]
        tab[:, K + p, :] = sums[3 * NS : 4 * NS] + sums[4 * NS : 5 * NS] + sums[5 * NS : 6 * NS]

    def route(d):
        to = lax.rem(sl + d, NS)
        return pltpu.make_async_remote_copy(
            src_ref=tab.at[to], dst_ref=orx.at[sl], send_sem=os_sem.at[d], recv_sem=or_sem.at[sl],
            device_id={"slab": to}, device_id_type=MESH,
        )

    def route_from(d):
        to = lax.rem(sl + d, NS)
        return pltpu.make_async_remote_copy(
            src_ref=tab.at[to], dst_ref=orx.at[to], send_sem=os_sem.at[d], recv_sem=or_sem.at[to],
            device_id={"slab": to}, device_id_type=MESH,
        )

    @pl.loop(1, NS)
    def _(d):
        route(d).start()

    orx[sl] = tab[sl]

    for copy in halos:
        copy.wait_recv()
    tail = pl.ds(8 - HALO, HALO)
    expand(0, HALO, cr[1, 0, tail], cr[1, 1, tail], cr[1, 2, tail])
    expand(HALO + ROWS, HALO, cr[0, 0, 0:HALO], cr[0, 1, 0:HALO], cr[0, 2, 0:HALO])
    for step in range(STEPS):
        src, dst = states[step], states[step + 1]
        shift = -HALO if step == STEPS - 1 else 0
        advance(src, dst, cx, step + 1, HALO, shift)
        advance(src, dst, cx, HALO + ROWS - step - 1, HALO, shift)

    for k in range(EARLY):
        for d in ORDER:

            @pl.when(jnp.logical_or(at_edge(k, mem_peer(d)), mem_peer(d) >= PIECES * QS))
            def _():
                forward(k, d).start()

    @pl.loop(EARLY, K)
    def _(k):
        for d in ORDER:
            forward(k, d).start()

    @pl.loop(0, K)
    def _(k):
        recv[k, pl.ds(2 * me, 2)] = send[me * K + k]

    @pl.loop(1, NS)
    def _(d):
        route_from(d).wait_recv()

    totals = orx[0]
    for s in range(1, NS):
        totals = totals + orx[s]
    wtot[...] = totals[0:K]
    utot[...] = totals[K : 2 * K]

    def back(k, d):
        q = mem_peer(d)
        return pltpu.make_async_remote_copy(
            src_ref=ana.at[k, pl.ds(pl.multiple_of(q * ML, ML), ML)],
            dst_ref=ret.at[me, pl.ds(pl.multiple_of(k * ML, ML), ML)],
            send_sem=rs_sem.at[k, d], recv_sem=rr_sem.at[k, me],
            device_id={"mem": q}, device_id_type=MESH,
        )

    def back_from(k, d):
        q = mem_peer(d)
        return pltpu.make_async_remote_copy(
            src_ref=ana.at[k, pl.ds(pl.multiple_of(q * ML, ML), ML)],
            dst_ref=ret.at[q, pl.ds(pl.multiple_of(k * ML, ML), ML)],
            send_sem=rs_sem.at[k, d], recv_sem=rr_sem.at[k, q],
            device_id={"mem": q}, device_id_type=MESH,
        )

    eye = jnp.where(
        lax.broadcasted_iota(jnp.int32, (M, M), 0) == lax.broadcasted_iota(jnp.int32, (M, M), 1),
        1.0, 0.0,
    )

    @pl.loop(0, K)
    def _(k):
        @pl.loop(1, NM)
        def _(d):
            forward_from(k, d).wait_recv()

        x = recv[k].reshape(M, W)
        mean = jnp.sum(x, axis=0, keepdims=True) * (1.0 / M)
        spread = (x - mean).astype(BF16)
        weight = wtot[pl.ds(k, 1), :]
        weighted = (spread.astype(F32) * weight).astype(BF16)
        system = (M - 1.0) * eye + nt(weighted, spread)
        squares = jnp.sum(jnp.sum(system * system, axis=0, keepdims=True), axis=1, keepdims=True)
        scale = 8.0 * jnp.sqrt(squares * (1.0 / M))
        pull = row_times(utot[pl.ds(k, 1), :] - weight * mean, spread)
        iterate = (system * (1.0 / scale)).astype(BF16)
        root = (1.5 * eye - 0.5 * iterate.astype(F32)).astype(BF16)
        iterate = nn(iterate, root).astype(BF16)
        for sweep in range(1, NS_STEPS):
            factor = (1.5 * eye - 0.5 * nn(root, iterate)).astype(BF16)
            if sweep < NS_STEPS - 1:
                iterate = nn(iterate, factor).astype(BF16)
            root = nn(factor, root).astype(BF16)
        gain = row_times(row_times(pull, root), root) * (1.0 / scale)
        transform = (jnp.sqrt((M - 1.0) / scale) * root.astype(F32) + gain).astype(BF16)
        ana[k] = mean + nn(transform, spread)
        for d in ORDER:
            back(k, d).start()
        ret[me, pl.ds(pl.multiple_of(k * ML, ML), ML), :] = ana[
            k, pl.ds(pl.multiple_of(me * ML, ML), ML), :
        ]

    @pl.loop(0, K)
    def _(k):
        @pl.loop(1, NM)
        def _(d):
            back_from(k, d).wait_recv()

    @pl.loop(0, ML)
    def _(m):
        for q in range(NM):
            out_ref[m, q * 8 : q * 8 + 8, :] = ret[q, pl.ds(m, K, stride=ML), :]

    for copy in halos:
        copy.wait_send()

    @pl.loop(1, NS)
    def _(d):
        route(d).wait_send()

    @pl.loop(0, K)
    def _(k):
        @pl.loop(1, NM)
        def _(d):
            forward(k, d).wait_send()
            back(k, d).wait_send()


def shards(ensemble, diffusivity, velocity, obs_value, obs_weight, obs_slab, obs_cell):
    vmem = pl.BlockSpec(memory_space=pltpu.VMEM)
    dma = pltpu.SemaphoreType.DMA
    return pl.pallas_call(
        kernel,
        out_shape=jax.ShapeDtypeStruct((ML, NM * K, W), F32),
        in_specs=[pl.BlockSpec(memory_space=pltpu.HBM)] * 7,
        out_specs=vmem,
        scratch_shapes=[
            pltpu.VMEM((ML * ROWS, W), F32),
            pltpu.VMEM((NM * K, W), F32),
            pltpu.VMEM((2, NM * K, W), F32),
            pltpu.VMEM((OBS // W, W), F32),
            pltpu.VMEM((OBS // W, W), F32),
            pltpu.VMEM((1, OBS), jnp.int32),
            pltpu.VMEM((OBS // W, W), jnp.int32),
            pltpu.VMEM((ROWS + 2 * HALO, 2, 8, W), F32),
            pltpu.VMEM((ROWS + 2 * HALO, 2, 8, W), F32),
            pltpu.VMEM((ROWS + 2 * HALO, 2, 8, W), F32),
            pltpu.VMEM((ROWS + 2 * HALO, 2, 8, W), F32),
            pltpu.VMEM((5, ROWS + 2 * HALO, 8, W), F32),
            pltpu.VMEM((2, 3, 8, W), F32),
            pltpu.VMEM((2, 3, 8, W), F32),
            pltpu.VMEM((ROWS, 2, 8, W), F32),
            pltpu.VMEM((K, 2 * NM, 8, W), F32),
            pltpu.VMEM((K, M, W), F32),
            pltpu.VMEM((NM, K * ML, W), F32),
            pltpu.VMEM((NS, 2 * K, W), F32),
            pltpu.VMEM((NS, 2 * K, W), F32),
            pltpu.VMEM((K, W), F32),
            pltpu.VMEM((K, W), F32),
            dma((7,)),
            dma((2,)),
            dma((2,)),
            dma((2,)),
            dma((2,)),
            dma((K, NM)),
            dma((K, NM)),
            dma((K, NM)),
            dma((K, NM)),
            dma((NS,)),
            dma((NS,)),
        ],
        compiler_params=pltpu.CompilerParams(
            collective_id=0, has_side_effects=True, vmem_limit_bytes=62 * 2**20
        ),
    )(
        ensemble.reshape(ML * ROWS, W),
        diffusivity,
        velocity,
        obs_value.reshape(OBS // W, W),
        obs_weight.reshape(OBS // W, W),
        obs_slab.reshape(1, OBS),
        obs_cell.reshape(OBS // W, W),
    )


def solution(mesh):
    return jax.shard_map(
        shards,
        mesh=mesh,
        in_specs=(
            P("mem", "slab", None),
            P("slab", None),
            P(None, "slab", None),
            P(("mem", "slab")),
            P(("mem", "slab")),
            P(("mem", "slab"), None),
            P(("mem", "slab")),
        ),
        out_specs=P("mem", "slab", None),
        check_vma=False,
    )
```

```python
import jax
import jax.numpy as jnp
from jax import lax
from jax.experimental import pallas as pl
from jax.experimental.pallas import tpu as pltpu
from jax.sharding import PartitionSpec as P

STEPS = 4
NS_STEPS = 5
NM = 16
NS = 32
K = 8
M = 256
ML = 16
W = 128
OBS = 1280
ROWS = 128
HALO = 4
GF, GB = 4, 4
FG, BG, PAIRS = K // GF, K // GB, K // 2
EARLY = 1
PIECES, STRIDE, QS = 3, 40, 5
MESH = pl.DeviceIdType.MESH
F32 = jnp.float32
BF16 = jnp.bfloat16
ORDER = (8, 7, 9, 6, 10, 5, 11, 4, 12, 3, 13, 2, 14, 1, 15)


def dot(a, b, dims):
    return lax.dot_general(a, b, (dims, ((), ())), preferred_element_type=F32)


def nn(a, b):
    return dot(a, b, ((1,), (0,)))


def nt(a, b):
    return dot(a, b, ((1,), (1,)))


def parts(x):
    hi = x.astype(BF16).astype(F32)
    rest = x - hi
    mid = rest.astype(BF16).astype(F32)
    return hi, mid, rest - mid


def row_times(row, mat_t):
    hi, mid, lo = parts(row)
    n = row.shape[1]
    at = lax.broadcasted_iota(jnp.int32, (16, n), 0)
    stack = jnp.where(at == 0, hi, jnp.where(at == 1, mid, jnp.where(at == 2, lo, 0.0)))
    return jnp.sum(nt(stack.astype(BF16), mat_t), axis=0, keepdims=True)


def advance(src, dst, cx, at, rows, shift=0):
    for r in range(rows):
        c = [cx[i, at + r] for i in range(5)]
        for h in range(2):
            x = src[at + r, h]
            dst[at + r + shift, h] = (
                (c[0] * x + c[3] * src[at + r - 1, h])
                + (c[4] * src[at + r + 1, h] + c[1] * pltpu.roll(x, W - 1, 1))
                + c[2] * pltpu.roll(x, 1, 1)
            )


def combine(d, vx, vy):
    ax, ay = 0.5 * vx, 0.5 * vy
    return 1.0 - 4.0 * d, d - ax, d + ax, d + ay, d - ay


def kernel(
    ens_hbm, dif_hbm, vel_hbm, val_hbm, wt_hbm, slab_hbm, cell_hbm, out_ref,
    ens, dif_ref, vel_ref, val_ref, wt_ref, slab_ref, cell_ref, b0, b1, b2, b3, cx, cs, cr, send, recv, ana, ret, tab, orx, wtot, utot,
    in_sem, hs_sem, hr_sem, cs_sem, cr_sem, fs_sem, fr_sem, rs_sem, rr_sem, os_sem, or_sem,
):
    me = lax.axis_index("mem")
    sl = lax.axis_index("slab")

    def mem_peer(d):
        return lax.rem(me + d, NM)

    pairs = (
        (dif_hbm, dif_ref), (vel_hbm, vel_ref), (ens_hbm, ens),
        (wt_hbm, wt_ref), (val_hbm, val_ref), (slab_hbm, slab_ref), (cell_hbm, cell_ref),
    )
    loads = [pltpu.make_async_copy(a, b, in_sem.at[i]) for i, (a, b) in enumerate(pairs)]
    for load in loads:
        load.start()
    bar = pltpu.get_barrier_semaphore()

    @pl.loop(1, NM)
    def _(d):
        pl.semaphore_signal(bar, inc=1, device_id={"mem": mem_peer(d)}, device_id_type=MESH)

    @pl.loop(1, NS)
    def _(d):
        pl.semaphore_signal(
            bar, inc=1, device_id={"slab": lax.rem(sl + d, NS)}, device_id_type=MESH
        )

    loads[0].wait()
    loads[1].wait()
    for i, ref in enumerate((dif_ref, vel_ref.at[0], vel_ref.at[1])):
        cs[0, i] = ref[0:8]
        cs[1, i] = ref[120:128]

    def expand(at, rows, d, vx, vy):
        for i, c in enumerate(combine(d, vx, vy)):
            cx[i, pl.ds(at, rows)] = jnp.broadcast_to(c[:, None, :], (rows, 8, W))

    @pl.loop(0, NM)
    def _(b):
        own = pl.ds(pl.multiple_of(b * 8, 8), 8)
        expand(HALO + b * 8, 8, dif_ref[own], vel_ref[0, own], vel_ref[1, own])

    loads[2].wait()

    @pl.loop(0, NM)
    def _(b):
        for h in range(2):
            tiles = [
                ens[pl.ds(pl.multiple_of((h * 8 + m) * ROWS + b * 8, 8), 8), :] for m in range(8)
            ]
            b0[pl.ds(HALO + b * 8, 8), h] = jnp.swapaxes(jnp.stack(tiles, axis=0), 0, 1)

    up = lax.rem(sl + NS - 1, NS)
    down = lax.rem(sl + 1, NS)

    def halo(side, to):
        start, land = ((HALO, HALO + ROWS), (ROWS, 0))[side]
        fields = pltpu.make_async_remote_copy(
            src_ref=b0.at[pl.ds(start, HALO)], dst_ref=b0.at[pl.ds(land, HALO)],
            send_sem=hs_sem.at[side], recv_sem=hr_sem.at[side],
            device_id={"slab": to}, device_id_type=MESH,
        )
        coeffs = pltpu.make_async_remote_copy(
            src_ref=cs.at[side], dst_ref=cr.at[side],
            send_sem=cs_sem.at[side], recv_sem=cr_sem.at[side],
            device_id={"slab": to}, device_id_type=MESH,
        )
        return fields, coeffs

    halos = halo(0, up) + halo(1, down)

    def forward(k, d):
        q = mem_peer(d)
        return pltpu.make_async_remote_copy(
            src_ref=send.at[pl.ds(q * K + GF * k, GF)], dst_ref=recv.at[k, me],
            send_sem=fs_sem.at[k, d], recv_sem=fr_sem.at[k, me],
            device_id={"mem": q}, device_id_type=MESH,
        )

    def forward_from(k, d):
        q = mem_peer(d)
        return pltpu.make_async_remote_copy(
            src_ref=send.at[pl.ds(q * K + GF * k, GF)], dst_ref=recv.at[k, q],
            send_sem=fs_sem.at[k, d], recv_sem=fr_sem.at[k, q],
            device_id={"mem": q}, device_id_type=MESH,
        )

    def at_edge(k, q):
        low = q == 0 if GF * k < HALO else False
        high = q == NM - 1 if GF * (k + 1) > HALO else False
        return jnp.logical_or(low, high)

    states = (b0, b1, b2, b3, send)

    @pl.loop(0, PIECES)
    def _(b):
        for step in range(STEPS):
            first = HALO + step + 1
            rows = ROWS - 2 * step - 2 - (PIECES - 1) * STRIDE
            shift = -HALO if step == STEPS - 1 else 0
            advance(states[step], states[step + 1], cx, first + b * STRIDE, rows, shift)

        @pl.when(b == 0)
        def _():
            pl.semaphore_wait(bar, NM - 1 + NS - 1)
            for copy in halos:
                copy.start()

        for k in range(EARLY):
            for i in range(QS):
                q = b * QS + i

                @pl.when(jnp.logical_and(q != me, jnp.logical_not(at_edge(k, q))))
                def _():
                    forward(k, lax.rem(q - me + NM, NM)).start()

    for load in loads[3:]:
        load.wait()

    def row(ref):
        return jnp.concatenate([ref[i : i + 1, :] for i in range(OBS // W)], axis=1)

    wt, val, cell = row(wt_ref), row(val_ref), row(cell_ref)
    mine = lax.broadcasted_iota(jnp.int32, (NS, OBS), 0) == slab_ref[...]
    rows = [jnp.where(mine, piece, 0.0) for piece in parts(wt) + parts(wt * val)]
    left = jnp.concatenate(rows, axis=0).astype(BF16)
    column = lax.broadcasted_iota(jnp.int32, (W, OBS), 0)
    for p in range(K):
        hot = jnp.where(column + p * W == cell, 1.0, 0.0).astype(BF16)
        sums = nt(left, hot)
        tab[:, p, :] = sums[0:NS] + sums[NS : 2 * NS] + sums[2 * NS : 3 * NS]
        tab[:, K + p, :] = sums[3 * NS : 4 * NS] + sums[4 * NS : 5 * NS] + sums[5 * NS : 6 * NS]

    def route(d):
        to = lax.rem(sl + d, NS)
        return pltpu.make_async_remote_copy(
            src_ref=tab.at[to], dst_ref=orx.at[sl], send_sem=os_sem.at[d], recv_sem=or_sem.at[sl],
            device_id={"slab": to}, device_id_type=MESH,
        )

    def route_from(d):
        to = lax.rem(sl + d, NS)
        return pltpu.make_async_remote_copy(
            src_ref=tab.at[to], dst_ref=orx.at[to], send_sem=os_sem.at[d], recv_sem=or_sem.at[to],
            device_id={"slab": to}, device_id_type=MESH,
        )

    @pl.loop(1, NS)
    def _(d):
        route(d).start()

    orx[sl] = tab[sl]

    for copy in halos:
        copy.wait_recv()
    tail = pl.ds(8 - HALO, HALO)
    expand(0, HALO, cr[1, 0, tail], cr[1, 1, tail], cr[1, 2, tail])
    expand(HALO + ROWS, HALO, cr[0, 0, 0:HALO], cr[0, 1, 0:HALO], cr[0, 2, 0:HALO])
    for step in range(STEPS):
        src, dst = states[step], states[step + 1]
        shift = -HALO if step == STEPS - 1 else 0
        advance(src, dst, cx, step + 1, HALO, shift)
        advance(src, dst, cx, HALO + ROWS - step - 1, HALO, shift)

    for k in range(EARLY):
        for d in ORDER:

            @pl.when(jnp.logical_or(at_edge(k, mem_peer(d)), mem_peer(d) >= PIECES * QS))
            def _():
                forward(k, d).start()

    @pl.loop(EARLY, FG)
    def _(k):
        for d in ORDER:
            forward(k, d).start()

    @pl.loop(0, FG)
    def _(k):
        recv[k, me] = send[pl.ds(me * K + GF * k, GF)]

    @pl.loop(1, NS)
    def _(d):
        route_from(d).wait_recv()

    totals = orx[0]
    for s in range(1, NS):
        totals = totals + orx[s]
    wtot[...] = totals[0:K]
    utot[...] = totals[K : 2 * K]

    def back(k, d):
        q = mem_peer(d)
        return pltpu.make_async_remote_copy(
            src_ref=ana.at[k, q], dst_ref=ret.at[me, pl.ds(pl.multiple_of(k * GB * ML, GB * ML), GB * ML)],
            send_sem=rs_sem.at[k, d], recv_sem=rr_sem.at[k, me],
            device_id={"mem": q}, device_id_type=MESH,
        )

    def back_from(k, d):
        q = mem_peer(d)
        return pltpu.make_async_remote_copy(
            src_ref=ana.at[k, q], dst_ref=ret.at[q, pl.ds(pl.multiple_of(k * GB * ML, GB * ML), GB * ML)],
            send_sem=rs_sem.at[k, d], recv_sem=rr_sem.at[k, q],
            device_id={"mem": q}, device_id_type=MESH,
        )

    eye = jnp.where(
        lax.broadcasted_iota(jnp.int32, (M, M), 0) == lax.broadcasted_iota(jnp.int32, (M, M), 1),
        1.0, 0.0,
    )

    def one_and_half(product):
        return (1.5 * eye - 0.5 * product).astype(BF16)

    @pl.loop(0, PAIRS)
    def _(k):
        group = k // (GF // 2)
        place = 2 * (k % (GF // 2))

        @pl.when(place == 0)
        def _():
            @pl.loop(1, NM)
            def _(d):
                forward_from(group, d).wait_recv()

        two = range(2)
        x = [recv[group, :, place + j].reshape(M, W) for j in two]
        mean = [jnp.sum(x[j], axis=0, keepdims=True) * (1.0 / M) for j in two]
        spread = [(x[j] - mean[j]).astype(BF16) for j in two]
        weight = [wtot[pl.ds(2 * k + j, 1), :] for j in two]
        weighted = [(spread[j].astype(F32) * weight[j]).astype(BF16) for j in two]
        system = [(M - 1.0) * eye + nt(weighted[j], spread[j]) for j in two]
        squares = [
            jnp.sum(jnp.sum(a * a, axis=0, keepdims=True), axis=1, keepdims=True) for a in system
        ]
        scale = [8.0 * jnp.sqrt(a * (1.0 / M)) for a in squares]
        pull = [
            row_times(utot[pl.ds(2 * k + j, 1), :] - weight[j] * mean[j], spread[j]) for j in two
        ]
        iterate = [(system[j] * (1.0 / scale[j])).astype(BF16) for j in two]
        root = [one_and_half(iterate[j].astype(F32)) for j in two]
        iterate = [nn(iterate[j], root[j]).astype(BF16) for j in two]
        for sweep in range(1, NS_STEPS):
            factor = [one_and_half(nn(root[j], iterate[j])) for j in two]
            if sweep < NS_STEPS - 1:
                iterate = [nn(iterate[j], factor[j]).astype(BF16) for j in two]
            root = [nn(factor[j], root[j]).astype(BF16) for j in two]
        first = [row_times(pull[j], root[j]) for j in two]
        gain = [row_times(first[j], root[j]) * (1.0 / scale[j]) for j in two]
        for j in two:
            transform = (jnp.sqrt((M - 1.0) / scale[j]) * root[j].astype(F32) + gain[j]).astype(BF16)
            result = mean[j] + nn(transform, spread[j])
            at = (2 * (k % (GB // 2)) + j) * ML
            ana[k // (GB // 2), :, pl.ds(pl.multiple_of(at, ML), ML)] = result.reshape(NM, ML, W)

        @pl.when(k % (GB // 2) == GB // 2 - 1)
        def _():
            out = k // (GB // 2)
            for d in ORDER:
                back(out, d).start()
            ret[me, pl.ds(pl.multiple_of(out * GB * ML, GB * ML), GB * ML), :] = ana[out, me]

    @pl.loop(0, BG)
    def _(k):
        @pl.loop(1, NM)
        def _(d):
            back_from(k, d).wait_recv()

    @pl.loop(0, ML)
    def _(m):
        for q in range(NM):
            out_ref[m, q * 8 : q * 8 + 8, :] = ret[q, pl.ds(m, K, stride=ML), :]

    for copy in halos:
        copy.wait_send()

    @pl.loop(1, NS)
    def _(d):
        route(d).wait_send()

    @pl.loop(1, NM)
    def _(d):
        @pl.loop(0, FG)
        def _(k):
            forward(k, d).wait_send()

        @pl.loop(0, BG)
        def _(k):
            back(k, d).wait_send()


def shards(ensemble, diffusivity, velocity, obs_value, obs_weight, obs_slab, obs_cell):
    vmem = pl.BlockSpec(memory_space=pltpu.VMEM)
    dma = pltpu.SemaphoreType.DMA
    return pl.pallas_call(
        kernel,
        out_shape=jax.ShapeDtypeStruct((ML, NM * K, W), F32),
        in_specs=[pl.BlockSpec(memory_space=pltpu.HBM)] * 7,
        out_specs=vmem,
        scratch_shapes=[
            pltpu.VMEM((ML * ROWS, W), F32),
            pltpu.VMEM((NM * K, W), F32),
            pltpu.VMEM((2, NM * K, W), F32),
            pltpu.VMEM((OBS // W, W), F32),
            pltpu.VMEM((OBS // W, W), F32),
            pltpu.VMEM((1, OBS), jnp.int32),
            pltpu.VMEM((OBS // W, W), jnp.int32),
            pltpu.VMEM((ROWS + 2 * HALO, 2, 8, W), F32),
            pltpu.VMEM((ROWS + 2 * HALO, 2, 8, W), F32),
            pltpu.VMEM((ROWS + 2 * HALO, 2, 8, W), F32),
            pltpu.VMEM((ROWS + 2 * HALO, 2, 8, W), F32),
            pltpu.VMEM((5, ROWS + 2 * HALO, 8, W), F32),
            pltpu.VMEM((2, 3, 8, W), F32),
            pltpu.VMEM((2, 3, 8, W), F32),
            pltpu.VMEM((ROWS, 2, 8, W), F32),
            pltpu.VMEM((FG, NM, GF, 2, 8, W), F32),
            pltpu.VMEM((BG, NM, GB * ML, W), F32),
            pltpu.VMEM((NM, K * ML, W), F32),
            pltpu.VMEM((NS, 2 * K, W), F32),
            pltpu.VMEM((NS, 2 * K, W), F32),
            pltpu.VMEM((K, W), F32),
            pltpu.VMEM((K, W), F32),
            dma((7,)),
            dma((2,)),
            dma((2,)),
            dma((2,)),
            dma((2,)),
            dma((FG, NM)),
            dma((FG, NM)),
            dma((BG, NM)),
            dma((BG, NM)),
            dma((NS,)),
            dma((NS,)),
        ],
        compiler_params=pltpu.CompilerParams(
            collective_id=0, has_side_effects=True, vmem_limit_bytes=62 * 2**20
        ),
    )(
        ensemble.reshape(ML * ROWS, W),
        diffusivity,
        velocity,
        obs_value.reshape(OBS // W, W),
        obs_weight.reshape(OBS // W, W),
        obs_slab.reshape(1, OBS),
        obs_cell.reshape(OBS // W, W),
    )


def solution(mesh):
    return jax.shard_map(
        shards,
        mesh=mesh,
        in_specs=(
            P("mem", "slab", None),
            P("slab", None),
            P(None, "slab", None),
            P(("mem", "slab")),
            P(("mem", "slab")),
            P(("mem", "slab"), None),
            P(("mem", "slab")),
        ),
        out_specs=P("mem", "slab", None),
        check_vma=False,
    )
```

```python
import jax
import jax.numpy as jnp
from jax import lax
from jax.experimental import pallas as pl
from jax.experimental.pallas import tpu as pltpu
from jax.sharding import PartitionSpec as P

STEPS = 4
NS_STEPS = 5
NM = 16
NS = 32
K = 8
M = 256
ML = 16
W = 128
OBS = 1280
ROWS = 128
HALO = 4
GF, GB = 4, 4
FG, BG, PAIRS = K // GF, K // GB, K // 2
BACK = ((0, 0, 64), (1, 0, 32), (1, 32, 32))
QB = 8
EARLY = 1
PIECES, STRIDE, QS = 3, 40, 5
MESH = pl.DeviceIdType.MESH
F32 = jnp.float32
BF16 = jnp.bfloat16
ORDER = (8, 7, 9, 6, 10, 5, 11, 4, 12, 3, 13, 2, 14, 1, 15)


def dot(a, b, dims):
    return lax.dot_general(a, b, (dims, ((), ())), preferred_element_type=F32)


def nn(a, b):
    return dot(a, b, ((1,), (0,)))


def nt(a, b):
    return dot(a, b, ((1,), (1,)))


def parts(x):
    hi = x.astype(BF16).astype(F32)
    rest = x - hi
    mid = rest.astype(BF16).astype(F32)
    return hi, mid, rest - mid


def row_times(row, mat_t):
    hi, mid, lo = parts(row)
    n = row.shape[1]
    at = lax.broadcasted_iota(jnp.int32, (16, n), 0)
    stack = jnp.where(at == 0, hi, jnp.where(at == 1, mid, jnp.where(at == 2, lo, 0.0)))
    return jnp.sum(nt(stack.astype(BF16), mat_t), axis=0, keepdims=True)


def advance(src, dst, cx, at, rows, shift=0):
    for r in range(rows):
        c = [cx[i, at + r] for i in range(5)]
        for h in range(2):
            x = src[at + r, h]
            dst[at + r + shift, h] = (
                (c[0] * x + c[3] * src[at + r - 1, h])
                + (c[4] * src[at + r + 1, h] + c[1] * pltpu.roll(x, W - 1, 1))
                + c[2] * pltpu.roll(x, 1, 1)
            )


def combine(d, vx, vy):
    ax, ay = 0.5 * vx, 0.5 * vy
    return 1.0 - 4.0 * d, d - ax, d + ax, d + ay, d - ay


def kernel(
    ens_hbm, dif_hbm, vel_hbm, val_hbm, wt_hbm, slab_hbm, cell_hbm, ret,
    ens, dif_ref, vel_ref, val_ref, wt_ref, slab_ref, cell_ref, b0, b1, b2, b3, cx, cs, cr, send, recv, ana, tab, orx, wtot, utot,
    in_sem, hs_sem, hr_sem, cs_sem, cr_sem, fs_sem, fr_sem, rs_sem, rr_sem, os_sem, or_sem, own_sem,
):
    me = lax.axis_index("mem")
    sl = lax.axis_index("slab")

    def mem_peer(d):
        return lax.rem(me + d, NM)

    pairs = (
        (dif_hbm, dif_ref), (vel_hbm, vel_ref), (ens_hbm, ens),
        (wt_hbm, wt_ref), (val_hbm, val_ref), (slab_hbm, slab_ref), (cell_hbm, cell_ref),
    )
    loads = [pltpu.make_async_copy(a, b, in_sem.at[i]) for i, (a, b) in enumerate(pairs)]
    for load in loads:
        load.start()
    bar = pltpu.get_barrier_semaphore()

    @pl.loop(1, NM)
    def _(d):
        pl.semaphore_signal(bar, inc=1, device_id={"mem": mem_peer(d)}, device_id_type=MESH)

    @pl.loop(1, NS)
    def _(d):
        pl.semaphore_signal(
            bar, inc=1, device_id={"slab": lax.rem(sl + d, NS)}, device_id_type=MESH
        )

    loads[0].wait()
    loads[1].wait()
    for i, ref in enumerate((dif_ref, vel_ref.at[0], vel_ref.at[1])):
        cs[0, i] = ref[0:8]
        cs[1, i] = ref[120:128]

    def expand(at, rows, d, vx, vy):
        for i, c in enumerate(combine(d, vx, vy)):
            cx[i, pl.ds(at, rows)] = jnp.broadcast_to(c[:, None, :], (rows, 8, W))

    @pl.loop(0, NM)
    def _(b):
        own = pl.ds(pl.multiple_of(b * 8, 8), 8)
        expand(HALO + b * 8, 8, dif_ref[own], vel_ref[0, own], vel_ref[1, own])

    loads[2].wait()

    @pl.loop(0, NM)
    def _(b):
        for h in range(2):
            tiles = [
                ens[pl.ds(pl.multiple_of((h * 8 + m) * ROWS + b * 8, 8), 8), :] for m in range(8)
            ]
            b0[pl.ds(HALO + b * 8, 8), h] = jnp.swapaxes(jnp.stack(tiles, axis=0), 0, 1)

    up = lax.rem(sl + NS - 1, NS)
    down = lax.rem(sl + 1, NS)

    def halo(side, to):
        start, land = ((HALO, HALO + ROWS), (ROWS, 0))[side]
        fields = pltpu.make_async_remote_copy(
            src_ref=b0.at[pl.ds(start, HALO)], dst_ref=b0.at[pl.ds(land, HALO)],
            send_sem=hs_sem.at[side], recv_sem=hr_sem.at[side],
            device_id={"slab": to}, device_id_type=MESH,
        )
        coeffs = pltpu.make_async_remote_copy(
            src_ref=cs.at[side], dst_ref=cr.at[side],
            send_sem=cs_sem.at[side], recv_sem=cr_sem.at[side],
            device_id={"slab": to}, device_id_type=MESH,
        )
        return fields, coeffs

    halos = halo(0, up) + halo(1, down)

    def forward(k, d):
        q = mem_peer(d)
        return pltpu.make_async_remote_copy(
            src_ref=send.at[pl.ds(q * K + GF * k, GF)], dst_ref=recv.at[k, me],
            send_sem=fs_sem.at[k, d], recv_sem=fr_sem.at[k, me],
            device_id={"mem": q}, device_id_type=MESH,
        )

    def forward_from(k, d):
        q = mem_peer(d)
        return pltpu.make_async_remote_copy(
            src_ref=send.at[pl.ds(q * K + GF * k, GF)], dst_ref=recv.at[k, q],
            send_sem=fs_sem.at[k, d], recv_sem=fr_sem.at[k, q],
            device_id={"mem": q}, device_id_type=MESH,
        )

    def at_edge(k, q):
        low = q == 0 if GF * k < HALO else False
        high = q == NM - 1 if GF * (k + 1) > HALO else False
        return jnp.logical_or(low, high)

    states = (b0, b1, b2, b3, send)

    @pl.loop(0, PIECES)
    def _(b):
        for step in range(STEPS):
            first = HALO + step + 1
            rows = ROWS - 2 * step - 2 - (PIECES - 1) * STRIDE
            shift = -HALO if step == STEPS - 1 else 0
            advance(states[step], states[step + 1], cx, first + b * STRIDE, rows, shift)

        @pl.when(b == 0)
        def _():
            pl.semaphore_wait(bar, NM - 1 + NS - 1)
            for copy in halos:
                copy.start()

        for k in range(EARLY):
            for i in range(QS):
                q = b * QS + i

                @pl.when(jnp.logical_and(q != me, jnp.logical_not(at_edge(k, q))))
                def _():
                    forward(k, lax.rem(q - me + NM, NM)).start()

    for load in loads[3:]:
        load.wait()

    def row(ref):
        return jnp.concatenate([ref[i : i + 1, :] for i in range(OBS // W)], axis=1)

    wt, val, cell = row(wt_ref), row(val_ref), row(cell_ref)
    mine = lax.broadcasted_iota(jnp.int32, (NS, OBS), 0) == slab_ref[...]
    rows = [jnp.where(mine, piece, 0.0) for piece in parts(wt) + parts(wt * val)]
    left = jnp.concatenate(rows, axis=0).astype(BF16)
    column = lax.broadcasted_iota(jnp.int32, (W, OBS), 0)
    for p in range(K):
        hot = jnp.where(column + p * W == cell, 1.0, 0.0).astype(BF16)
        sums = nt(left, hot)
        tab[:, p, :] = sums[0:NS] + sums[NS : 2 * NS] + sums[2 * NS : 3 * NS]
        tab[:, K + p, :] = sums[3 * NS : 4 * NS] + sums[4 * NS : 5 * NS] + sums[5 * NS : 6 * NS]

    def route(d):
        to = lax.rem(sl + d, NS)
        return pltpu.make_async_remote_copy(
            src_ref=tab.at[to], dst_ref=orx.at[sl], send_sem=os_sem.at[d], recv_sem=or_sem.at[sl],
            device_id={"slab": to}, device_id_type=MESH,
        )

    def route_from(d):
        to = lax.rem(sl + d, NS)
        return pltpu.make_async_remote_copy(
            src_ref=tab.at[to], dst_ref=orx.at[to], send_sem=os_sem.at[d], recv_sem=or_sem.at[to],
            device_id={"slab": to}, device_id_type=MESH,
        )

    @pl.loop(1, NS)
    def _(d):
        route(d).start()

    orx[sl] = tab[sl]

    for copy in halos:
        copy.wait_recv()
    tail = pl.ds(8 - HALO, HALO)
    expand(0, HALO, cr[1, 0, tail], cr[1, 1, tail], cr[1, 2, tail])
    expand(HALO + ROWS, HALO, cr[0, 0, 0:HALO], cr[0, 1, 0:HALO], cr[0, 2, 0:HALO])
    for step in range(STEPS):
        src, dst = states[step], states[step + 1]
        shift = -HALO if step == STEPS - 1 else 0
        advance(src, dst, cx, step + 1, HALO, shift)
        advance(src, dst, cx, HALO + ROWS - step - 1, HALO, shift)

    for k in range(EARLY):
        for d in ORDER:

            @pl.when(jnp.logical_or(at_edge(k, mem_peer(d)), mem_peer(d) >= PIECES * QS))
            def _():
                forward(k, d).start()

    @pl.loop(EARLY, FG)
    def _(k):
        for d in ORDER:
            forward(k, d).start()

    @pl.loop(0, FG)
    def _(k):
        recv[k, me] = send[pl.ds(me * K + GF * k, GF)]

    @pl.loop(1, NS)
    def _(d):
        route_from(d).wait_recv()

    totals = orx[0]
    for s in range(1, NS):
        totals = totals + orx[s]
    wtot[...] = totals[0:K]
    utot[...] = totals[K : 2 * K]

    def back_by(n, d, source):
        k, start, rows = BACK[n]
        q = mem_peer(d)
        land = pl.ds(k * GB * ML + start, rows)
        return pltpu.make_async_remote_copy(
            src_ref=ana.at[k, q, pl.ds(start, rows)], dst_ref=ret.at[source, land],
            send_sem=rs_sem.at[n, d], recv_sem=rr_sem.at[n, source],
            device_id={"mem": q}, device_id_type=MESH,
        )

    def back(n, d):
        return back_by(n, d, me)

    def back_from(n, d):
        return back_by(n, d, mem_peer(d))

    def own(k):
        place = pl.ds(pl.multiple_of(k * GB * ML, GB * ML), GB * ML)
        return pltpu.make_async_copy(ana.at[k, me], ret.at[me, place], own_sem.at[k])

    eye = jnp.where(
        lax.broadcasted_iota(jnp.int32, (M, M), 0) == lax.broadcasted_iota(jnp.int32, (M, M), 1),
        1.0, 0.0,
    )

    def one_and_half(product):
        return (1.5 * eye - 0.5 * product).astype(BF16)

    @pl.loop(0, PAIRS)
    def _(k):
        group = k // (GF // 2)
        place = 2 * (k % (GF // 2))

        @pl.when(place == 0)
        def _():
            @pl.loop(1, NM)
            def _(d):
                forward_from(group, d).wait_recv()

        two = range(2)
        x = [recv[group, :, place + j].reshape(M, W) for j in two]
        mean = [jnp.sum(x[j], axis=0, keepdims=True) * (1.0 / M) for j in two]
        spread = [(x[j] - mean[j]).astype(BF16) for j in two]
        weight = [wtot[pl.ds(2 * k + j, 1), :] for j in two]
        weighted = [(spread[j].astype(F32) * weight[j]).astype(BF16) for j in two]
        system = [(M - 1.0) * eye + nt(weighted[j], spread[j]) for j in two]
        squares = [
            jnp.sum(jnp.sum(a * a, axis=0, keepdims=True), axis=1, keepdims=True) for a in system
        ]
        scale = [8.0 * jnp.sqrt(a * (1.0 / M)) for a in squares]
        pull = [
            row_times(utot[pl.ds(2 * k + j, 1), :] - weight[j] * mean[j], spread[j]) for j in two
        ]
        iterate = [(system[j] * (1.0 / scale[j])).astype(BF16) for j in two]
        root = [one_and_half(iterate[j].astype(F32)) for j in two]
        iterate = [nn(iterate[j], root[j]).astype(BF16) for j in two]
        for sweep in range(1, NS_STEPS):
            factor = [one_and_half(nn(root[j], iterate[j])) for j in two]
            if sweep < NS_STEPS - 1:
                iterate = [nn(iterate[j], factor[j]).astype(BF16) for j in two]
            root = [nn(factor[j], root[j]).astype(BF16) for j in two]
        first = [row_times(pull[j], root[j]) for j in two]
        gain = [row_times(first[j], root[j]) * (1.0 / scale[j]) for j in two]
        for j in two:
            transform = (jnp.sqrt((M - 1.0) / scale[j]) * root[j].astype(F32) + gain[j]).astype(BF16)
            result = mean[j] + nn(transform, spread[j])
            at = (2 * (k % (GB // 2)) + j) * ML
            ana[k // (GB // 2), :, pl.ds(pl.multiple_of(at, ML), ML)] = result.reshape(NM, ML, W)

        for n in range(len(BACK)):

            @pl.when(k == n + 1)
            def _():
                for d in ORDER:
                    back(n, d).start()

        @pl.when(k % 2 == 1)
        def _():
            own(k // 2).start()

    for n in range(len(BACK)):

        @pl.loop(1, NM)
        def _(d):
            back_from(n, d).wait_recv()

    @pl.loop(0, BG)
    def _(k):
        own(k).wait()

    for copy in halos:
        copy.wait_send()

    @pl.loop(1, NS)
    def _(d):
        route(d).wait_send()

    @pl.loop(1, NM)
    def _(d):
        @pl.loop(0, FG)
        def _(k):
            forward(k, d).wait_send()

        for n in range(len(BACK)):
            back(n, d).wait_send()


def reorder(in_ref, out_ref):
    for m in range(ML):
        for q in range(QB):
            out_ref[m, q * K : q * K + K, :] = in_ref[q, pl.ds(m, K, stride=ML), :]


def shards(ensemble, diffusivity, velocity, obs_value, obs_weight, obs_slab, obs_cell):
    dma = pltpu.SemaphoreType.DMA
    landed = pl.pallas_call(
        kernel,
        out_shape=jax.ShapeDtypeStruct((NM, K * ML, W), F32),
        in_specs=[pl.BlockSpec(memory_space=pltpu.HBM)] * 7,
        out_specs=pl.BlockSpec(memory_space=pltpu.HBM),
        scratch_shapes=[
            pltpu.VMEM((ML * ROWS, W), F32),
            pltpu.VMEM((NM * K, W), F32),
            pltpu.VMEM((2, NM * K, W), F32),
            pltpu.VMEM((OBS // W, W), F32),
            pltpu.VMEM((OBS // W, W), F32),
            pltpu.VMEM((1, OBS), jnp.int32),
            pltpu.VMEM((OBS // W, W), jnp.int32),
            pltpu.VMEM((ROWS + 2 * HALO, 2, 8, W), F32),
            pltpu.VMEM((ROWS + 2 * HALO, 2, 8, W), F32),
            pltpu.VMEM((ROWS + 2 * HALO, 2, 8, W), F32),
            pltpu.VMEM((ROWS + 2 * HALO, 2, 8, W), F32),
            pltpu.VMEM((5, ROWS + 2 * HALO, 8, W), F32),
            pltpu.VMEM((2, 3, 8, W), F32),
            pltpu.VMEM((2, 3, 8, W), F32),
            pltpu.VMEM((ROWS, 2, 8, W), F32),
            pltpu.VMEM((FG, NM, GF, 2, 8, W), F32),
            pltpu.VMEM((BG, NM, GB * ML, W), F32),
            pltpu.VMEM((NS, 2 * K, W), F32),
            pltpu.VMEM((NS, 2 * K, W), F32),
            pltpu.VMEM((K, W), F32),
            pltpu.VMEM((K, W), F32),
            dma((7,)),
            dma((2,)),
            dma((2,)),
            dma((2,)),
            dma((2,)),
            dma((FG, NM)),
            dma((FG, NM)),
            dma((len(BACK), NM)),
            dma((len(BACK), NM)),
            dma((NS,)),
            dma((NS,)),
            dma((BG,)),
        ],
        compiler_params=pltpu.CompilerParams(
            collective_id=0, has_side_effects=True, vmem_limit_bytes=62 * 2**20
        ),
    )(
        ensemble.reshape(ML * ROWS, W),
        diffusivity,
        velocity,
        obs_value.reshape(OBS // W, W),
        obs_weight.reshape(OBS // W, W),
        obs_slab.reshape(1, OBS),
        obs_cell.reshape(OBS // W, W),
    )
    return pl.pallas_call(
        reorder,
        grid=(NM // QB,),
        in_specs=[pl.BlockSpec((QB, K * ML, W), lambda i: (i, 0, 0))],
        out_specs=pl.BlockSpec((ML, QB * K, W), lambda i: (0, i, 0)),
        out_shape=jax.ShapeDtypeStruct((ML, NM * K, W), F32),
        compiler_params=pltpu.CompilerParams(vmem_limit_bytes=62 * 2**20),
    )(landed)


def solution(mesh):
    return jax.shard_map(
        shards,
        mesh=mesh,
        in_specs=(
            P("mem", "slab", None),
            P("slab", None),
            P(None, "slab", None),
            P(("mem", "slab")),
            P(("mem", "slab")),
            P(("mem", "slab"), None),
            P(("mem", "slab")),
        ),
        out_specs=P("mem", "slab", None),
        check_vma=False,
    )
```
